32 devices in a mesh: row: 8 (over z, y), col: 4 (over x, core).
Axes of the slice: x: 2, y: 2, z: 4, core: 2. Of those that a mesh axis runs over, the one named last changes fastest.
Arguments:
- window: float32 [2048, 8192], P('row', 'col'), may hold values from -6 to 6
- leaf_y: float32 [2, 2048, 256], P(None, 'row', 'col'), may hold values from -6 to 6
- tree_y: float32 [2, 3, 2048, 256], P(None, None, 'row', 'col'), may hold values from -6 to 6
Outputs:
- updated: float32 [2048, 8192], P('row', 'col')
The draws below stay inside these ranges and needn't reach their ends.
All inputs are finite; a program needn't handle non-finite values.
Results may differ from the reference program's by a relative error of at most 0.0003.
Values sent between devices are 32-bit elements; how exact they have to be, the bound alone decides.
No kernel may reach another device: no remote copies, remote signals or barrier semaphores. Data moves between devices by JAX's collectives and lax.ppermute only.
A program may use at most 128 MiB of HBM per device.

```python
import jax
import jax.numpy as jnp
import numpy as np
from jax import lax

B = 256
NC = 8192
R = 256
M = 2048
LEVELS = 3
N_ROW = 8


def shard_levels(stream_key, dims, shards, low, largest):
    gain, own = 1.0, jax.random.fold_in(stream_key, 6)
    for axis_at, blocks in shards:
        steps = jnp.exp(jax.random.uniform(jax.random.fold_in(own, axis_at), (blocks,), jnp.float32, low / len(shards), largest / len(shards)))
        gain = gain * jnp.repeat(steps, dims[axis_at] // blocks).reshape([-1 if axis == axis_at else 1 for axis in range(len(dims))])
    return gain


def normal_values(stream_key, dims, deviation, limit, cuts=(), held_as=jnp.bfloat16):
    drawn = deviation * jax.random.normal(stream_key, dims, jnp.float32)
    if cuts:
        drawn = drawn * shard_levels(stream_key, dims, cuts, -0.22, 0.18)
    return jnp.clip(drawn, -limit, limit).astype(held_as)


def setup_inputs(seed: int = 0) -> dict:
    arg_keys = jax.random.split(jax.random.key(seed), 4)
    return {
        "window": normal_values(arg_keys[0], (M, NC), 1.0, 6.0, ((0, 8), (1, 4)), jnp.float32),
        "leaf_y": normal_values(arg_keys[1], (2, M, B), 1.0, 6.0, ((1, 8), (2, 4)), jnp.float32),
        "tree_y": normal_values(arg_keys[2], (2, LEVELS, N_ROW * B, B), 1.0, 6.0, ((2, 8), (3, 4)), jnp.float32),
    }


def triangle(gramian):
    return jnp.triu(gramian, 1) + jnp.diag(jnp.diag(gramian)) * 0.5

def reflect(matrix_block, vectors, gramian, inners):
    coefficients = jax.scipy.linalg.solve_triangular(triangle(gramian), inners, trans=1, lower=False)
    return matrix_block - jnp.dot(vectors.astype(jnp.float32), coefficients.astype(jnp.float32), precision=lax.Precision.HIGHEST, preferred_element_type=jnp.float32)

def leaf_step(paired):
    matrix_block, vectors = paired
    gramian = jnp.dot(vectors.T.astype(jnp.float32), vectors.astype(jnp.float32), precision=lax.Precision.HIGHEST, preferred_element_type=jnp.float32)
    inners = jnp.dot(vectors.T.astype(jnp.float32), matrix_block.astype(jnp.float32), precision=lax.Precision.HIGHEST, preferred_element_type=jnp.float32)
    return reflect(matrix_block, vectors, gramian, inners)

def reference(window, leaf_y, tree_y):
    blocks = window.reshape(N_ROW, R, NC)
    for panel_index in range(2):
        vectors = leaf_y[panel_index].reshape(N_ROW, R, B)
        blocks = lax.map(leaf_step, (blocks, vectors))
        for level_index in range(LEVELS):
            partner = np.arange(N_ROW) ^ 1 << level_index
            tree_vectors = tree_y[panel_index, level_index].reshape(N_ROW, B, B)
            top_rows = blocks[:, :B]
            gramians = jnp.einsum('nki,nkj->nij', tree_vectors, tree_vectors, precision=lax.Precision.HIGHEST)
            inners = jnp.einsum('nki,nkj->nij', tree_vectors, top_rows, precision=lax.Precision.HIGHEST)
            gram_total = gramians + gramians[partner]
            inner_total = inners + inners[partner]
            new_top = jax.vmap(reflect)(top_rows, tree_vectors, gram_total, inner_total)
            blocks = blocks.at[:, :B].set(new_top)
    return blocks.reshape(N_ROW * R, NC)
```

```python
import functools

import jax
import jax.numpy as jnp
from jax import lax
from jax.experimental import pallas as pl
from jax.experimental.pallas import tpu as pltpu
from jax.sharding import PartitionSpec as P

F32, BF16 = jnp.float32, jnp.bfloat16
NN, NT = ((1,), (0,)), ((1,), (1,))
CHUNKS = 2
VMEM_BYTES = 50 * 2**20


def halves(value):
    high = value.astype(BF16)
    return high, (value - high.astype(F32)).astype(BF16)


def dot(left, right, dims):
    return lax.dot_general(left, right, (dims, ((), ())), preferred_element_type=F32)


def multiply(left, right, dims=NN):
    (left_high, left_low), (right_high, right_low) = left, right
    return dot(left_high, right_high, dims) + (
        dot(left_high, right_low, dims) + dot(left_low, right_high, dims)
    )


def iotas(rows, columns):
    shape = (rows, columns)
    return lax.broadcasted_iota(jnp.int32, shape, 0), lax.broadcasted_iota(jnp.int32, shape, 1)


def spread(compact, mask):
    times = mask.shape[0] // compact.shape[0]
    full = compact if times == 1 else jnp.concatenate([compact] * times, 0)
    return jnp.where(mask, full, 0.0)


def triangle_inverses(gramians):
    width = gramians[0].shape[0]
    size = min(width, 32)
    row, column = iotas(width, width)
    scaled = []
    for gramian in gramians:
        diagonal = jnp.where(row == column, gramian, 0.0)
        across = 1.0 / jnp.sqrt(0.5 * jnp.sum(diagonal, 0, keepdims=True))
        down = 1.0 / jnp.sqrt(0.5 * jnp.sum(diagonal, 1, keepdims=True))
        scaled.append((jnp.where(row < column, gramian * down * across, 0.0), across, down))
    small_row, small_column = iotas(size, width)
    unit = jnp.where(small_row == small_column % size, 1.0, 0.0)
    mask = row // size == column // size
    inverses = []
    stacks = []
    for upper, _, _ in scaled:
        block = jnp.where(mask, -upper, 0.0)
        compact = block[:size]
        for start in range(size, width, size):
            compact = compact + block[start : start + size]
        stacks.append((unit + compact, multiply(halves(compact), halves(block))))
    reach = 2
    while reach < size:
        last = reach * 2 >= size
        following = []
        for inverse, power in stacks:
            left = inverse if last else jnp.concatenate([inverse, power], 0)
            both = multiply(halves(left), halves(spread(power, mask)))
            following.append((inverse + both[:size], None if last else both[size:]))
        stacks = following
        reach *= 2
    inverses = [inverse for inverse, _ in stacks]
    while size < width:
        small_row, small_column = iotas(size, width)
        even = (small_column // size) % 2 == 0
        block_row, block_column = row // size, column // size
        mask = block_row == block_column
        beside = (block_row % 2 == 0) & (block_column == block_row + 1)
        following = []
        for inverse, (upper, _, _) in zip(inverses, scaled):
            top = jnp.where(even, inverse, 0.0)
            step = multiply(halves(top), halves(jnp.where(beside, upper, 0.0)))
            step = multiply(halves(step), halves(spread(inverse, mask)))
            following.append(jnp.concatenate([top - step, inverse - top], 0))
        inverses = following
        size *= 2
    return [(inverse, across, down) for inverse, (_, across, down) in zip(inverses, scaled)]


def reflectors_of(vectors_t, inverse):
    solved, across, down = inverse
    return multiply(halves((vectors_t * down).T), halves(solved), NT) * across


def store(high_ref, low_ref, index, value):
    high_ref[index], low_ref[index] = halves(value)


def operator(high_ref, low_ref, *index):
    return (high_ref[index], low_ref[index]) if index else (high_ref[...], low_ref[...])


def assemble(position, near_ref, far_ref, columns, group, block, into, index):
    half = len(columns) // 2
    width = near_ref.shape[-2]
    for at, offset in enumerate(columns):
        ref = near_ref if at < half else far_ref
        where = pl.multiple_of((position ^ offset) * width, width)
        into[(*index, pl.ds(where, width), slice(None))] = ref[at % half, group, block]


def home_gramians(columns, low, position_ref, near_ref, far_ref, vectors_ref, send_ref):
    position = position_ref[0]
    shard = near_ref.shape[-2]
    for block in range(vectors_ref.shape[0]):
        assemble(position, near_ref, far_ref, columns, 0, block, vectors_ref, (block,))
    width = vectors_ref.shape[1]
    for level in range(low):
        first, second = halves(vectors_ref[1 + level]), halves(vectors_ref[1 + low + level])
        send_ref[level, :width] = multiply(first, first, NT)
        own = vectors_ref[1 + low + level, pl.ds(pl.multiple_of(position * shard, shard), shard), :]
        send_ref[level, width:] = multiply(halves(own), second, NT)


def home_leaf(has_next, vectors_ref, high_ref, low_ref):
    vectors_t = vectors_ref[0]
    pair = halves(vectors_t)
    (inverse,) = triangle_inverses([multiply(pair, pair, NT)])
    width = vectors_t.shape[1]
    row, column = iotas(width, width)
    step = multiply(halves(reflectors_of(vectors_t, inverse)), pair)
    leaf = jnp.where(row == column, 1.0, 0.0) - step
    rows = leaf.shape[0]
    high_ref[:rows], low_ref[:rows] = halves(leaf)
    if has_next:
        high_ref[rows:], low_ref[rows:] = halves(multiply(halves(vectors_ref[1]), halves(leaf)))


def home_tree(low, vectors_ref, own_ref, far_ref, high_ref, low_ref):
    width = vectors_ref.shape[1]
    sums = [own_ref[level, :width] + far_ref[level, :width] for level in range(low)]
    for level, inverse in enumerate(triangle_inverses(sums)):
        store(high_ref, low_ref, level, reflectors_of(vectors_ref[1 + level], inverse))


def top_tree(columns, places, blocks, position_ref, near_ref, far_ref, *refs):
    yt_high, yt_low, v_high, v_low, vectors = refs
    position = position_ref[0]
    groups, levels = len(places), len(blocks)
    sums = []
    for level, block in enumerate(blocks):
        apart = 2**level
        gramians = []
        for group in range(groups):
            assemble(position, near_ref, far_ref, columns, places[group], block, vectors, (level, group))
            pair = halves(vectors[level, group])
            yt_high[level, group], yt_low[level, group] = pair
            gramians.append(multiply(pair, pair, NT))
        sums += [gramians[g] + gramians[g ^ apart] for g in range(groups) if g < g ^ apart]
    inverses = iter(triangle_inverses(sums))
    for level in range(levels):
        apart = 2**level
        for group in range(groups):
            if group < group ^ apart:
                inverse = next(inverses)
                for member in (group, group ^ apart):
                    store(v_high, v_low, (level, member), reflectors_of(vectors[level, member], inverse))


def top_leaf(columns, places, low, position_ref, near_ref, far_ref, *refs):
    a_high, a_low, yt_high, yt_low, vectors = refs
    position = position_ref[0]
    width = vectors.shape[-1]
    gramians = []
    for group, where in enumerate(places):
        assemble(position, near_ref, far_ref, columns, where, 0, vectors, (group, 0))
        pair = halves(vectors[group, 0])
        gramians.append(multiply(pair, pair, NT))
        for level in range(low):
            assemble(position, near_ref, far_ref, columns, where, 1 + level, vectors, (group, 1))
            store(yt_high, yt_low, (level, group), vectors[group, 1])
    row, column = iotas(vectors.shape[-1], vectors.shape[-1])
    for group, inverse in enumerate(triangle_inverses(gramians)):
        vectors_t = vectors[group, 0]
        step = multiply(halves(reflectors_of(vectors_t, inverse)), halves(vectors_t))
        store(a_high, a_low, group, jnp.where(row == column, 1.0, 0.0) - step)


def top_low(columns, places, low, position_ref, near_ref, far_ref, gram_near, gram_far, *refs):
    v_high, v_low, vectors, gramians = refs
    position = position_ref[0]
    for level in range(low):
        for group, where in enumerate(places):
            assemble(position, near_ref, far_ref, columns, where, 1 + level, vectors, (group,))
            assemble(position, gram_near, gram_far, columns, where, level, gramians, (group,))
        inverses = triangle_inverses([gramians[group] for group in range(len(places))])
        for group, inverse in enumerate(inverses):
            store(v_high, v_low, (level, group), reflectors_of(vectors[group], inverse))


def home_start(window_ref, high_ref, low_ref, out_ref, *inner_ref):
    both = multiply(operator(high_ref, low_ref), halves(window_ref[...]))
    rows = out_ref.shape[0]
    out_ref[...] = both[:rows]
    if inner_ref:
        inner_ref[0][...] = both[rows:]


def home_level(top_ref, own_ref, far_ref, v_high, v_low, yt_ref, out_ref, inner_ref):
    inner = own_ref[...] + far_ref[...]
    out = top_ref[...] - multiply(operator(v_high, v_low), halves(inner))
    out_ref[...] = out
    inner_ref[...] = multiply(halves(yt_ref[...]), halves(out))


def home_last(groups, position_ref, top_ref, own_ref, far_ref, v_high, v_low, *out_refs):
    width = top_ref.shape[1] // groups
    pair = operator(v_high, v_low)
    for group, out_ref in enumerate(out_refs):
        at = pl.ds(pl.multiple_of((position_ref[0] ^ group) * width, width), width)
        inner = own_ref[:, at] + far_ref[:, at]
        out_ref[...] = top_ref[:, at] - multiply(pair, halves(inner))


def top_levels(tops, levels, yt_high, yt_low, v_high, v_low):
    groups = len(tops)
    for level in range(levels):
        apart = 2**level
        inners = [multiply(operator(yt_high, yt_low, level, g), halves(tops[g])) for g in range(groups)]
        sums = [halves(inners[g] + inners[g ^ apart]) for g in range(groups) if g < g ^ apart]
        order = [g for g in range(groups) if g < g ^ apart]
        tops = [
            tops[g] - multiply(operator(v_high, v_low, level, g), sums[order.index(min(g, g ^ apart))])
            for g in range(groups)
        ]
    return tops


def middle(groups, levels, low, *refs):
    pieces, refs = refs[:groups], refs[groups:]
    yt_high, yt_low, v_high, v_low, a_high, a_low, e_high, e_low = refs[:8]
    out_ref = refs[8]
    tops = top_levels([ref[...] for ref in pieces], levels, yt_high, yt_low, v_high, v_low)
    for g in range(groups):
        top = multiply(operator(a_high, a_low, g), halves(tops[g]))
        out_ref[g] = top
        if low:
            refs[9][g] = multiply(operator(e_high, e_low, 0, g), halves(top))


def low_step(groups, level, top_ref, own_ref, far_ref, v_high, v_low, yt_high, yt_low, out_ref, inner_ref):
    for g in range(groups):
        inner = own_ref[g] + far_ref[g]
        top = top_ref[g] - multiply(operator(v_high, v_low, level, g), halves(inner))
        out_ref[g] = top
        inner_ref[g] = multiply(operator(yt_high, yt_low, level + 1, g), halves(top))


def finish(groups, levels, low, *refs):
    top_ref, refs = refs[0], refs[1:]
    tops = [top_ref[g] for g in range(groups)]
    if low:
        own_ref, far_ref, b_high, b_low = refs[:4]
        refs = refs[4:]
        tops = [
            tops[g] - multiply(operator(b_high, b_low, low - 1, g), halves(own_ref[g] + far_ref[g]))
            for g in range(groups)
        ]
    tops = top_levels(tops, levels, *refs[:4])
    for g, out_ref in enumerate(refs[4:]):
        out_ref[...] = tops[g]


def place(groups, chunks, position_ref, *refs):
    out_ref = refs[-1]
    width = refs[0].shape[1]
    for chunk in range(chunks):
        for g in range(groups):
            at = (chunk * groups + (position_ref[0] ^ g)) * width
            out_ref[:, pl.ds(pl.multiple_of(at, width), width)] = refs[chunk * groups + g][...]


def call(kernel, outs, operands, flops, scalars=0, scratch=()):
    in_memory = pl.BlockSpec(memory_space=pltpu.VMEM)
    specs = [pl.BlockSpec(memory_space=pltpu.SMEM)] * scalars + [in_memory] * (len(operands) - scalars)
    shapes = [jax.ShapeDtypeStruct(*out) for out in outs]
    moved = sum(x.size * x.dtype.itemsize for x in [*operands, *shapes])
    result = pl.pallas_call(
        kernel,
        out_shape=shapes,
        in_specs=specs,
        out_specs=[in_memory] * len(shapes),
        scratch_shapes=[pltpu.VMEM(*s) for s in scratch],
        compiler_params=pltpu.CompilerParams(vmem_limit_bytes=VMEM_BYTES),
        cost_estimate=pl.CostEstimate(flops=int(flops), bytes_accessed=int(moved), transcendentals=0),
    )(*operands)
    return result


def swapped(value, axis, mask):
    pairs = [(source, source ^ mask) for source in range(lax.axis_size(axis))]
    return lax.ppermute(value, axis, pairs)


def per_device(window, leaf_y, tree_y):
    rows, across = window.shape
    width = tree_y.shape[2]
    levels = lax.axis_size("row").bit_length() - 1
    top = min(2, levels)
    low = levels - top
    groups = 2**top
    row_at, col_at = lax.axis_index("row"), lax.axis_index("col")
    column_at = jnp.reshape(col_at, (1,)).astype(jnp.int32)
    group_at = jnp.reshape(row_at // 2**low, (1,)).astype(jnp.int32)
    col_masks = [2**bit for bit in reversed(range(lax.axis_size("col").bit_length() - 1))]
    columns = [0]
    for mask in col_masks:
        columns = columns + [offset ^ mask for offset in columns]
    unit = 2 * width**3 * 3

    leaf_t, tree_t = jnp.swapaxes(leaf_y, 1, 2), jnp.swapaxes(tree_y, 2, 3)

    def over_col(value):
        for mask in col_masks[:-1]:
            value = jnp.concatenate([value, swapped(value, "col", mask)], 0)
        return value, swapped(value, "col", col_masks[-1])

    order = [0]
    for bit in reversed(range(top)):
        order = order + [offset ^ 2**bit for offset in order]
    places = [order.index(offset) for offset in range(groups)]

    home_shard = jnp.concatenate([leaf_t[:1], tree_t[0, :low], tree_t[1, :low]], 0)
    home_near, home_far = over_col(home_shard[None, None])

    def over_all(value):
        value = value[None]
        for bit in reversed(range(top)):
            value = jnp.concatenate([value, swapped(value, "row", 2 ** (low + bit))], 0)
        return over_col(value[None])

    first_near, first_far = over_all(tree_t[0, low:])
    second_near, second_far = over_all(jnp.concatenate([leaf_t[1:], tree_t[1]], 0))

    blocks = home_shard.shape[0]
    vectors, sends = call(
        functools.partial(home_gramians, columns, low),
        [((blocks, width, rows), F32), ((max(low, 1), width + home_shard.shape[1], width), F32)],
        [column_at, home_near, home_far],
        unit * 2 * max(low, 1),
        scalars=1,
    )
    a_high, a_low = call(
        functools.partial(home_leaf, low > 0),
        [((rows + (width if low else 0), rows), BF16)] * 2,
        [vectors],
        unit * 8,
    )
    if low:
        fars = jnp.stack([swapped(sends[level], "row", 2**level) for level in range(low)])
        v_high, v_low = call(
            functools.partial(home_tree, low),
            [((low, rows, width), BF16)] * 2,
            [vectors, sends, fars],
            unit * 6 * low,
        )
        gram_shard = sends[:, width:] + fars[:, width:]
        gram_near, gram_far = over_all(gram_shard)

    kept = [((top, groups, width, rows), BF16)] * 2 + [((top, groups, rows, width), BF16)] * 2
    scratch = [((top, groups, width, rows), F32)]
    first_ops = call(
        functools.partial(top_tree, columns, places, list(range(top))),
        kept,
        [column_at, first_near, first_far],
        unit * 28,
        scalars=1,
        scratch=scratch,
    )
    leaf_ops = call(
        functools.partial(top_leaf, columns, places, low),
        [((groups, rows, rows), BF16)] * 2 + [((max(low, 1), groups, width, rows), BF16)] * 2,
        [column_at, second_near, second_far],
        unit * 32,
        scalars=1,
        scratch=[((groups, 2, width, rows), F32)],
    )
    if low:
        low_ops = call(
            functools.partial(top_low, columns, places, low),
            [((low, groups, rows, width), BF16)] * 2,
            [column_at, second_near, second_far, gram_near, gram_far],
            unit * 20 * low,
            scalars=1,
            scratch=[((groups, width, rows), F32), ((groups, width, width), F32)],
        )
    second_ops = call(
        functools.partial(top_tree, columns, places, [1 + low + l for l in range(top)]),
        kept,
        [column_at, second_near, second_far],
        unit * 28,
        scalars=1,
        scratch=scratch,
    )

    chunks = max(1, min(CHUNKS, across // groups // 128))
    wide = across // chunks
    narrow = wide // groups
    work = unit * wide // width
    piece = ((rows, narrow), F32)
    stack = ((groups, rows, narrow), F32)
    whole = ((rows, wide), F32)
    inner = ((width, wide), F32)
    results = []
    for chunk in range(chunks):
        part = window[:, chunk * wide : (chunk + 1) * wide]
        if low:
            here, own = call(home_start, [whole, inner], [part, a_high, a_low], work * 2)
            for level in range(low):
                far = swapped(own, "row", 2**level)
                if level < low - 1:
                    here, own = call(
                        home_level,
                        [whole, inner],
                        [here, own, far, v_high[level], v_low[level], vectors[2 + level]],
                        work * 2,
                    )
            pieces = call(
                functools.partial(home_last, groups),
                [piece] * groups,
                [group_at, here, own, far, v_high[low - 1], v_low[low - 1]],
                work,
                scalars=1,
            )
        else:
            (here,) = call(home_start, [whole], [part, a_high, a_low], work)
            pieces = [
                lax.dynamic_slice_in_dim(here, (group_at[0] ^ g) * narrow, narrow, 1) for g in range(groups)
            ]
        pieces = [pieces[0]] + [swapped(pieces[g], "row", g << low) for g in range(1, groups)]
        if low:
            here, own = call(
                functools.partial(middle, groups, top, low),
                [stack, ((groups, width, narrow), F32)],
                [*pieces, *first_ops, *leaf_ops],
                work * 6,
            )
            for level in range(low):
                far = swapped(own, "row", 2**level)
                if level < low - 1:
                    here, own = call(
                        functools.partial(low_step, groups, level),
                        [stack, ((groups, width, narrow), F32)],
                        [here, own, far, *low_ops, *leaf_ops[2:]],
                        work * 2,
                    )
            operands = [here, own, far, *low_ops, *second_ops]
        else:
            (here,) = call(
                functools.partial(middle, groups, top, low), [stack], [*pieces, *first_ops, *leaf_ops], work * 5
            )
            operands = [here, *second_ops]
        pieces = call(functools.partial(finish, groups, top, low), [piece] * groups, operands, work * 5)
        results += [pieces[0]] + [swapped(pieces[g], "row", g << low) for g in range(1, groups)]
    (updated,) = call(
        functools.partial(place, groups, chunks), [((rows, across), F32)], [group_at, *results], 0, scalars=1
    )
    return updated


def solution(mesh):
    return jax.shard_map(
        per_device,
        mesh=mesh,
        in_specs=(P("row", "col"), P(None, "row", "col"), P(None, None, "row", "col")),
        out_specs=P("row", "col"),
        check_vma=False,
    )
```

```python
import functools
import math

import jax
import jax.numpy as jnp
from jax import lax
from jax.experimental import pallas as pl
from jax.experimental.pallas import tpu as pltpu
from jax.sharding import PartitionSpec as P

F32, BF16 = jnp.float32, jnp.bfloat16
NN, NT = ((1,), (0,)), ((1,), (1,))
CHUNKS = 2
SPARE_BYTES = 8 * 2**20
COST = 1.0


def halves(value):
    high = value.astype(BF16)
    return high, (value - high.astype(F32)).astype(BF16)


def dot(left, right, dims):
    return lax.dot_general(left, right, (dims, ((), ())), preferred_element_type=F32)


def multiply(left, right, dims=NN):
    (left_high, left_low), (right_high, right_low) = left, right
    return dot(left_high, right_high, dims) + (
        dot(left_high, right_low, dims) + dot(left_low, right_high, dims)
    )


def iotas(rows, columns):
    shape = (rows, columns)
    return lax.broadcasted_iota(jnp.int32, shape, 0), lax.broadcasted_iota(jnp.int32, shape, 1)


def spread(compact, mask):
    times = mask.shape[0] // compact.shape[0]
    full = compact if times == 1 else jnp.concatenate([compact] * times, 0)
    return jnp.where(mask, full, 0.0)


def triangle_inverses(gramians):
    width = gramians[0].shape[0]
    size = min(width, 32)
    row, column = iotas(width, width)
    scaled = []
    for gramian in gramians:
        diagonal = jnp.where(row == column, gramian, 0.0)
        across = 1.0 / jnp.sqrt(0.5 * jnp.sum(diagonal, 0, keepdims=True))
        down = 1.0 / jnp.sqrt(0.5 * jnp.sum(diagonal, 1, keepdims=True))
        scaled.append((jnp.where(row < column, gramian * down * across, 0.0), across, down))
    small_row, small_column = iotas(size, width)
    unit = jnp.where(small_row == small_column % size, 1.0, 0.0)
    mask = row // size == column // size
    inverses = []
    stacks = []
    for upper, _, _ in scaled:
        block = jnp.where(mask, -upper, 0.0)
        compact = block[:size]
        for start in range(size, width, size):
            compact = compact + block[start : start + size]
        stacks.append((unit + compact, multiply(halves(compact), halves(block))))
    reach = 2
    while reach < size:
        last = reach * 2 >= size
        following = []
        for inverse, power in stacks:
            left = inverse if last else jnp.concatenate([inverse, power], 0)
            both = multiply(halves(left), halves(spread(power, mask)))
            following.append((inverse + both[:size], None if last else both[size:]))
        stacks = following
        reach *= 2
    inverses = [inverse for inverse, _ in stacks]
    while size < width:
        small_row, small_column = iotas(size, width)
        even = (small_column // size) % 2 == 0
        block_row, block_column = row // size, column // size
        mask = block_row == block_column
        beside = (block_row % 2 == 0) & (block_column == block_row + 1)
        following = []
        for inverse, (upper, _, _) in zip(inverses, scaled):
            top = jnp.where(even, inverse, 0.0)
            step = multiply(halves(top), halves(jnp.where(beside, upper, 0.0)))
            step = multiply(halves(step), halves(spread(inverse, mask)))
            following.append(jnp.concatenate([top - step, inverse - top], 0))
        inverses = following
        size *= 2
    return [(inverse, across, down) for inverse, (_, across, down) in zip(inverses, scaled)]


def reflectors_of(vectors_t, inverse):
    solved, across, down = inverse
    return multiply(halves((vectors_t * down).T), halves(solved), NT) * across


def store(high_ref, low_ref, index, value):
    high_ref[index], low_ref[index] = halves(value)


def operator(high_ref, low_ref, *index):
    return (high_ref[index], low_ref[index]) if index else (high_ref[...], low_ref[...])


def pack(low, leaf_ref, tree_ref, home_ref, early_ref, late_ref):
    levels = tree_ref.shape[1]
    top = levels - low
    home_ref[0, 0] = leaf_ref[0]
    early_ref[0, top] = leaf_ref[1]
    for level in range(levels):
        if level < low:
            home_ref[0, 1 + level] = tree_ref[0, level]
            early_ref[0, top + 1 + level] = tree_ref[1, level]
        else:
            early_ref[0, level - low] = tree_ref[0, level]
            late_ref[0, level - low] = tree_ref[1, level]


def extend(own_ref, *refs):
    count = own_ref.shape[1]
    refs[-1][:, :count] = own_ref[...]
    for at, ref in enumerate(refs[:-1]):
        refs[-1][0, count + at] = ref[...]


def join(*refs):
    count = len(refs) // 3
    for at in range(count):
        own_ref, far_ref, out_ref = refs[2 * at], refs[2 * at + 1], refs[2 * count + at]
        size = own_ref.shape[0]
        out_ref[:size] = own_ref[...]
        out_ref[size:] = far_ref[...]


def assemble(columns, groups, place, position, near_ref, far_ref, into_ref):
    half = len(columns) // 2
    shard = near_ref.shape[-2]
    for at, offset in enumerate(columns):
        ref = near_ref if at < half else far_ref
        where = pl.multiple_of((position ^ offset) * shard, shard)
        into_ref[:, pl.ds(where, shard), :] = ref[at % half * groups + place]


def home_gramians(columns, low, position_ref, near_ref, far_ref, vectors_ref, send_ref):
    assemble(columns, 1, 0, position_ref[0], near_ref, far_ref, vectors_ref)
    for level in range(low):
        pair = halves(vectors_ref[1 + level])
        send_ref[level] = multiply(pair, pair, NT)


def home_leaf(low, vectors_ref, high_ref, low_ref):
    vectors_t = vectors_ref[0]
    pair = halves(vectors_t)
    (inverse,) = triangle_inverses([multiply(pair, pair, NT)])
    width, rows = vectors_t.shape
    row, column = iotas(rows, rows)
    leaf = jnp.where(row == column, 1.0, 0.0) - multiply(halves(reflectors_of(vectors_t, inverse)), pair)
    high_ref[:rows], low_ref[:rows] = halves(leaf)
    if low:
        high_ref[rows:], low_ref[rows:] = halves(multiply(halves(vectors_ref[1]), halves(leaf)))


def home_low(low, vectors_ref, own_ref, *refs):
    far_refs, (v_high, v_low) = refs[:low], refs[low:]
    sums = [own_ref[level] + far_refs[level][...] for level in range(low)]
    for level, inverse in enumerate(triangle_inverses(sums)):
        store(v_high, v_low, level, reflectors_of(vectors_ref[1 + level], inverse))


def home_start(chunk, window_ref, high_ref, low_ref, out_ref, *inner_refs):
    rows, wide = out_ref.shape
    result = multiply(operator(high_ref, low_ref), halves(window_ref[:, chunk * wide : (chunk + 1) * wide]))
    out_ref[...] = result[:rows]
    for inner_ref in inner_refs:
        inner_ref[...] = result[rows:]


def home_first(low, window_ref, high_ref, low_ref, vectors_ref, own_ref, *refs):
    far_refs, (v_high, v_low, out_ref, inner_ref) = refs[:low], refs[low:]
    home_low(low, vectors_ref, own_ref, *far_refs, v_high, v_low)
    home_start(0, window_ref, high_ref, low_ref, out_ref, inner_ref)


def tree_operators(held, yt_high, yt_low, v_high, v_low):
    levels, groups = yt_high.shape[:2]
    sums = []
    for level in range(levels):
        apart = 2**level
        gramians = []
        for group in range(groups):
            pair = halves(held(group, level))
            yt_high[level, group], yt_low[level, group] = pair
            gramians.append(multiply(pair, pair, NT))
        sums += [gramians[g] + gramians[g ^ apart] for g in range(groups) if g < g ^ apart]
    inverses = iter(triangle_inverses(sums))
    for level in range(levels):
        apart = 2**level
        for group in range(groups):
            if group < group ^ apart:
                inverse = next(inverses)
                for member in (group, group ^ apart):
                    store(v_high, v_low, (level, member), reflectors_of(held(member, level), inverse))


def top_tree(columns, places, position_ref, near_ref, far_ref, yt_high, yt_low, v_high, v_low, held_ref):
    groups = len(places)
    for group, place in enumerate(places):
        assemble(columns, groups, place, position_ref[0], near_ref, far_ref, held_ref.at[group])
    tree_operators(lambda group, level: held_ref[group, level], yt_high, yt_low, v_high, v_low)


def top_leaf(first, held_ref, a_high, a_low, yt_high, yt_low):
    groups = held_ref.shape[0]
    gramians = []
    for group in range(groups):
        pair = halves(held_ref[group, first])
        gramians.append(multiply(pair, pair, NT))
    row, column = iotas(*a_high.shape[1:])
    for group, inverse in enumerate(triangle_inverses(gramians)):
        vectors_t = held_ref[group, first]
        step = multiply(halves(reflectors_of(vectors_t, inverse)), halves(vectors_t))
        store(a_high, a_low, group, jnp.where(row == column, 1.0, 0.0) - step)
    for level in range(held_ref.shape[1] - first - 1):
        for group in range(groups):
            store(yt_high, yt_low, (level, group), held_ref[group, first + 1 + level])


def top_low(low, late_ref, held_ref, v_high, v_low):
    groups = held_ref.shape[0]
    first, partners = held_ref.shape[1] - low, late_ref.shape[1] - low
    for level in range(low):
        gramians = []
        for group in range(groups):
            pair, partner = halves(held_ref[group, first + level]), halves(late_ref[group, partners + level])
            gramians.append(multiply(pair, pair, NT) + multiply(partner, partner, NT))
        for group, inverse in enumerate(triangle_inverses(gramians)):
            store(v_high, v_low, (level, group), reflectors_of(held_ref[group, first + level], inverse))


def home_level(top_ref, own_ref, far_ref, v_high, v_low, yt_ref, out_ref, inner_ref):
    inner = own_ref[...] + far_ref[...]
    out = top_ref[...] - multiply(operator(v_high, v_low), halves(inner))
    out_ref[...] = out
    inner_ref[...] = multiply(halves(yt_ref[...]), halves(out))


def home_last(groups, position_ref, top_ref, own_ref, far_ref, v_high, v_low, *out_refs):
    width = top_ref.shape[1] // groups
    pair = operator(v_high, v_low)
    for group, out_ref in enumerate(out_refs):
        at = pl.ds(pl.multiple_of((position_ref[0] ^ group) * width, width), width)
        inner = own_ref[:, at] + far_ref[:, at]
        out_ref[...] = top_ref[:, at] - multiply(pair, halves(inner))


def top_levels(tops, levels, yt_high, yt_low, v_high, v_low):
    groups = len(tops)
    for level in range(levels):
        apart = 2**level
        inners = [multiply(operator(yt_high, yt_low, level, g), halves(tops[g])) for g in range(groups)]
        sums = [halves(inners[g] + inners[g ^ apart]) for g in range(groups) if g < g ^ apart]
        order = [g for g in range(groups) if g < g ^ apart]
        tops = [
            tops[g] - multiply(operator(v_high, v_low, level, g), sums[order.index(min(g, g ^ apart))])
            for g in range(groups)
        ]
    return tops


def middle(groups, levels, low, *refs):
    pieces, refs = refs[:groups], refs[groups:]
    yt_high, yt_low, v_high, v_low, a_high, a_low, e_high, e_low = refs[:8]
    out_ref = refs[8]
    tops = top_levels([ref[...] for ref in pieces], levels, yt_high, yt_low, v_high, v_low)
    for g in range(groups):
        top = multiply(operator(a_high, a_low, g), halves(tops[g]))
        out_ref[g] = top
        if low:
            refs[9][g] = multiply(operator(e_high, e_low, 0, g), halves(top))


def low_step(groups, level, top_ref, own_ref, far_ref, v_high, v_low, yt_high, yt_low, out_ref, inner_ref):
    for g in range(groups):
        inner = own_ref[g] + far_ref[g]
        top = top_ref[g] - multiply(operator(v_high, v_low, level, g), halves(inner))
        out_ref[g] = top
        inner_ref[g] = multiply(operator(yt_high, yt_low, level + 1, g), halves(top))


def finish(groups, levels, low, *refs):
    top_ref, refs = refs[0], refs[1:]
    tops = [top_ref[g] for g in range(groups)]
    if low:
        own_ref, far_ref, b_high, b_low = refs[:4]
        refs = refs[4:]
        tops = [
            tops[g] - multiply(operator(b_high, b_low, low - 1, g), halves(own_ref[g] + far_ref[g]))
            for g in range(groups)
        ]
    tops = top_levels(tops, levels, *refs[:4])
    for g, out_ref in enumerate(refs[4:]):
        out_ref[...] = tops[g]


def place(groups, chunks, position_ref, *refs):
    out_ref = refs[-1]
    width = refs[0].shape[1]
    for chunk in range(chunks):
        for g in range(groups):
            at = (chunk * groups + (position_ref[0] ^ g)) * width
            out_ref[:, pl.ds(pl.multiple_of(at, width), width)] = refs[chunk * groups + g][...]


class Order:
    def __init__(self):
        self.last = None

    def __call__(self, kernel, outs, operands, scalars=0, scratch=(), products=0):
        in_memory = pl.BlockSpec(memory_space=pltpu.VMEM)
        specs = [pl.BlockSpec(memory_space=pltpu.SMEM)] * scalars + [in_memory] * (len(operands) - scalars)
        shapes = [jax.ShapeDtypeStruct(*out) for out in outs]
        moved = sum(x.size * x.dtype.itemsize for x in [*operands, *shapes])
        held = moved + sum(4 * math.prod(shape) for shape in scratch)
        body = kernel
        if self.last is not None:
            operands, specs = [self.last, *operands], [pl.BlockSpec(memory_space=pl.ANY), *specs]
            body = lambda token, *refs: kernel(*refs)
        results = pl.pallas_call(
            body,
            out_shape=shapes,
            in_specs=specs,
            out_specs=[in_memory] * len(shapes),
            scratch_shapes=[pltpu.VMEM(shape, F32) for shape in scratch],
            name=kernel.func.__name__ if isinstance(kernel, functools.partial) else kernel.__name__,
            compiler_params=pltpu.CompilerParams(vmem_limit_bytes=held + SPARE_BYTES),
            cost_estimate=pl.CostEstimate(
                flops=int(COST * products * 6 * 256**3), bytes_accessed=int(COST * moved), transcendentals=0
            ),
        )(*operands)
        self.last = results[0]
        return results


def swapped(value, axis, mask):
    pairs = [(source, source ^ mask) for source in range(lax.axis_size(axis))]
    return lax.ppermute(value, axis, pairs)


class Gather:
    def __init__(self, value, steps):
        self.value, self.steps = value, list(steps)
        self.send()

    def send(self):
        self.far = swapped(self.value, *self.steps.pop(0))

    @staticmethod
    def step(call, *gathers):
        gathers = [gather for gather in gathers if gather.steps]
        if not gathers:
            return
        shapes = [((2 * g.value.shape[0], *g.value.shape[1:]), F32) for g in gathers]
        joined = call(join, shapes, [x for g in gathers for x in (g.value, g.far)])
        for gather, value in zip(gathers, joined):
            gather.value = value
            gather.send()


def per_device(window, leaf_y, tree_y):
    rows, across = window.shape
    width = tree_y.shape[2]
    groups, low = lax.axis_size("top"), lax.axis_size("low").bit_length() - 1
    top = groups.bit_length() - 1
    column_at = jnp.reshape(lax.axis_index("col"), (1,)).astype(jnp.int32)
    group_at = jnp.reshape(lax.axis_index("top"), (1,)).astype(jnp.int32)
    col_masks = [2**bit for bit in reversed(range(lax.axis_size("col").bit_length() - 1))]
    columns, places = [0], [0]
    for mask in col_masks:
        columns = columns + [offset ^ mask for offset in columns]
    for bit in reversed(range(top)):
        places = places + [offset ^ 2**bit for offset in places]
    places = [places.index(offset) for offset in range(groups)]
    col_steps = [("col", mask) for mask in col_masks]
    all_steps = [("top", 2**bit) for bit in reversed(range(top))] + col_steps
    call = Order()

    leaf_t, tree_t = jnp.swapaxes(leaf_y, 1, 2), jnp.swapaxes(tree_y, 2, 3)
    shard = leaf_t.shape[1]
    home, early, late = call(
        functools.partial(pack, low),
        [((1, count, shard, rows), F32) for count in (1 + low, top + 1 + low, top)],
        [leaf_t, tree_t],
    )
    home, early = Gather(home, col_steps), Gather(early, all_steps)
    partners = [swapped(early.value[0, top + 1 + level], "low", 2**level) for level in range(low)]
    while home.steps:
        Gather.step(call, home)
    vectors, sends = call(
        functools.partial(home_gramians, columns, low),
        [((1 + low, width, rows), F32), ((max(low, 1), width, width), F32)],
        [column_at, home.value, home.far],
        scalars=1,
        products=low,
    )
    leaf = call(
        functools.partial(home_leaf, low), [((rows + (width if low else 0), rows), BF16)] * 2, [vectors], products=8
    )
    chunks = max(1, min(CHUNKS, across // groups // 128))
    wide = across // chunks
    narrow = wide // groups
    piece, stack = ((rows, narrow), F32), ((groups, rows, narrow), F32)
    whole, inner = ((rows, wide), F32), ((width, wide), F32)
    unit = wide / width
    heres, owns, far_inners = [], [], []

    def start(chunk):
        if low and chunk == 0:
            fars = [swapped(sends[level], "low", 2**level) for level in range(low)]
            *low_reflectors, here, own = call(
                functools.partial(home_first, low),
                [((low, rows, width), BF16)] * 2 + [whole, inner],
                [window, *leaf, vectors, sends, *fars],
                products=8 + 2 * unit,
            )
            own = [own]
        else:
            low_reflectors = []
            here, *own = call(
                functools.partial(home_start, chunk), [whole, inner][: 1 + (low > 0)], [window, *leaf], products=2 * unit
            )
        heres.append(here)
        owns.extend(own)
        far_inners.extend(swapped(inner, "low", 1) for inner in own)
        return low_reflectors

    v_high, v_low = start(0) or (None, None)
    if low:
        (late,) = call(extend, [((1, top + low, shard, rows), F32)], [late, *partners])
    Gather.step(call, early)
    late = Gather(late, all_steps)
    Gather.step(call, early, late)

    def give(chunk):
        here = heres[chunk]
        if low:
            own, far = owns[chunk], far_inners[chunk]
            for level in range(low - 1):
                here, own = call(
                    home_level, [whole, inner], [here, own, far, v_high[level], v_low[level], vectors[2 + level]]
                )
                far = swapped(own, "low", 2 ** (level + 1))
            pieces = call(
                functools.partial(home_last, groups),
                [piece] * groups,
                [group_at, here, own, far, v_high[low - 1], v_low[low - 1]],
                scalars=1,
                products=unit,
            )
        else:
            pieces = [
                lax.dynamic_slice_in_dim(here, (group_at[0] ^ g) * narrow, narrow, 1) for g in range(groups)
            ]
        return [pieces[0]] + [swapped(pieces[g], "top", g) for g in range(1, groups)]

    def through(pieces):
        outs = [stack, ((groups, width, narrow), F32)][: 1 + (low > 0)]
        results = call(functools.partial(middle, groups, top, low), outs, [*pieces, *first_ops, *leaf_ops], products=6 * unit)
        return [*results, *([swapped(results[1], "low", 1)] if low else [])]

    def back(state):
        if low:
            here, own, far = state
            for level in range(low - 1):
                here, own = call(
                    functools.partial(low_step, groups, level),
                    [stack, ((groups, width, narrow), F32)],
                    [here, own, far, *low_ops, *leaf_ops[2:]],
                )
                far = swapped(own, "low", 2 ** (level + 1))
            state = [here, own, far, *low_ops]
        pieces = call(functools.partial(finish, groups, top, low), [piece] * groups, [*state, *second_ops], products=5 * unit)
        return [pieces[0]] + [swapped(pieces[g], "top", g) for g in range(1, groups)]

    kept = [((top, groups, width, rows), BF16)] * 2 + [((top, groups, rows, width), BF16)] * 2
    given, states = [], []
    for chunk in range(chunks):
        if chunk + 1 < chunks:
            start(chunk + 1)
        given.append(give(chunk))
        if chunk == 0:
            while early.steps:
                Gather.step(call, early, late)
            *first_ops, held = call(
                functools.partial(top_tree, columns, places),
                [*kept, ((groups, top + 1 + low, width, rows), F32)],
                [column_at, early.value, early.far],
                scalars=1,
                products=32,
            )
            leaf_ops = call(
                functools.partial(top_leaf, top),
                [((groups, rows, rows), BF16)] * 2 + [((max(low, 1), groups, width, rows), BF16)] * 2,
                [held],
                products=32,
            )
        else:
            states.append(through(given[chunk - 1]))
    while late.steps:
        Gather.step(call, late)
    *second_ops, late_held = call(
        functools.partial(top_tree, columns, places),
        [*kept, ((groups, top + low, width, rows), F32)],
        [column_at, late.value, late.far],
        scalars=1,
        products=32,
    )
    if low:
        low_ops = call(
            functools.partial(top_low, low), [((low, groups, rows, width), BF16)] * 2, [late_held, held], products=32 * low
        )
    states.append(through(given[-1]))
    results = []
    for state in states:
        results += back(state)
    (updated,) = call(
        functools.partial(place, groups, chunks), [((rows, across), F32)], [group_at, *results], scalars=1
    )
    return updated


def solution(mesh):
    count = mesh.shape["row"]
    groups = min(4, count)
    split = jax.sharding.Mesh(mesh.devices.reshape(groups, count // groups, -1), ("top", "low", "col"))
    row = ("top", "low")
    return jax.shard_map(
        per_device,
        mesh=split,
        in_specs=(P(row, "col"), P(None, row, "col"), P(None, None, row, "col")),
        out_specs=P(row, "col"),
        check_vma=False,
    )
```

```python
import functools
import math

import jax
import jax.numpy as jnp
from jax import lax
from jax.experimental import pallas as pl
from jax.experimental.pallas import tpu as pltpu
from jax.sharding import PartitionSpec as P

F32, BF16 = jnp.float32, jnp.bfloat16
NN, NT = ((1,), (0,)), ((1,), (1,))
CHUNKS = 2
SPARE_BYTES = 8 * 2**20
COST = 1.0


def halves(value):
    high = value.astype(BF16)
    return high, (value - high.astype(F32)).astype(BF16)


def dot(left, right, dims):
    return lax.dot_general(left, right, (dims, ((), ())), preferred_element_type=F32)


def multiply(left, right, dims=NN):
    (left_high, left_low), (right_high, right_low) = left, right
    return dot(left_high, right_high, dims) + (
        dot(left_high, right_low, dims) + dot(left_low, right_high, dims)
    )


def iotas(rows, columns):
    shape = (rows, columns)
    return lax.broadcasted_iota(jnp.int32, shape, 0), lax.broadcasted_iota(jnp.int32, shape, 1)


def spread(compact, mask):
    times = mask.shape[0] // compact.shape[0]
    full = compact if times == 1 else jnp.concatenate([compact] * times, 0)
    return jnp.where(mask, full, 0.0)


def triangle_inverses(gramians):
    width = gramians[0].shape[0]
    size = min(width, 32)
    row, column = iotas(width, width)
    scaled = []
    for gramian in gramians:
        diagonal = jnp.where(row == column, gramian, 0.0)
        across = 1.0 / jnp.sqrt(0.5 * jnp.sum(diagonal, 0, keepdims=True))
        down = 1.0 / jnp.sqrt(0.5 * jnp.sum(diagonal, 1, keepdims=True))
        scaled.append((jnp.where(row < column, gramian * down * across, 0.0), across, down))
    small_row, small_column = iotas(size, width)
    unit = jnp.where(small_row == small_column % size, 1.0, 0.0)
    mask = row // size == column // size
    inverses = []
    stacks = []
    for upper, _, _ in scaled:
        block = jnp.where(mask, -upper, 0.0)
        compact = block[:size]
        for start in range(size, width, size):
            compact = compact + block[start : start + size]
        stacks.append((unit + compact, multiply(halves(compact), halves(block))))
    reach = 2
    while reach < size:
        last = reach * 2 >= size
        following = []
        for inverse, power in stacks:
            left = inverse if last else jnp.concatenate([inverse, power], 0)
            both = multiply(halves(left), halves(spread(power, mask)))
            following.append((inverse + both[:size], None if last else both[size:]))
        stacks = following
        reach *= 2
    inverses = [inverse for inverse, _ in stacks]
    while size < width:
        small_row, small_column = iotas(size, width)
        even = (small_column // size) % 2 == 0
        block_row, block_column = row // size, column // size
        mask = block_row == block_column
        beside = (block_row % 2 == 0) & (block_column == block_row + 1)
        following = []
        for inverse, (upper, _, _) in zip(inverses, scaled):
            top = jnp.where(even, inverse, 0.0)
            step = multiply(halves(top), halves(jnp.where(beside, upper, 0.0)))
            step = multiply(halves(step), halves(spread(inverse, mask)))
            following.append(jnp.concatenate([top - step, inverse - top], 0))
        inverses = following
        size *= 2
    return [(inverse, across, down) for inverse, (_, across, down) in zip(inverses, scaled)]


def reflectors_of(vectors_t, inverse):
    solved, across, down = inverse
    return multiply(halves((vectors_t * down).T), halves(solved), NT) * across


def store(high_ref, low_ref, index, value):
    high_ref[index], low_ref[index] = halves(value)


def operator(high_ref, low_ref, *index):
    return (high_ref[index], low_ref[index]) if index else (high_ref[...], low_ref[...])


def pack(low, leaf_ref, tree_ref, home_ref, early_ref, late_ref):
    levels = tree_ref.shape[1]
    top = levels - low
    home_ref[0, 0] = leaf_ref[0]
    early_ref[0, top] = leaf_ref[1]
    for level in range(levels):
        if level < low:
            home_ref[0, 1 + level] = tree_ref[0, level]
            early_ref[0, top + 1 + level] = tree_ref[1, level]
        else:
            early_ref[0, level - low] = tree_ref[0, level]
            late_ref[0, level - low] = tree_ref[1, level]


def extend(own_ref, *refs):
    count = own_ref.shape[1]
    refs[-1][:, :count] = own_ref[...]
    for at, ref in enumerate(refs[:-1]):
        refs[-1][0, count + at] = ref[...]


def join(*refs):
    count = len(refs) // 3
    for at in range(count):
        own_ref, far_ref, out_ref = refs[2 * at], refs[2 * at + 1], refs[2 * count + at]
        size = own_ref.shape[0]
        out_ref[:size] = own_ref[...]
        out_ref[size:] = far_ref[...]


def assemble(columns, groups, place, position, near_ref, far_ref, into_ref):
    half = len(columns) // 2
    shard = near_ref.shape[-2]
    for at, offset in enumerate(columns):
        ref = near_ref if at < half else far_ref
        where = pl.multiple_of((position ^ offset) * shard, shard)
        into_ref[:, pl.ds(where, shard), :] = ref[at % half * groups + place]


def home_gramians(columns, low, position_ref, near_ref, far_ref, vectors_ref, send_ref):
    assemble(columns, 1, 0, position_ref[0], near_ref, far_ref, vectors_ref)
    for level in range(low):
        pair = halves(vectors_ref[1 + level])
        send_ref[level] = multiply(pair, pair, NT)


def home_leaf(low, vectors_ref, high_ref, low_ref):
    vectors_t = vectors_ref[0]
    pair = halves(vectors_t)
    (inverse,) = triangle_inverses([multiply(pair, pair, NT)])
    width, rows = vectors_t.shape
    row, column = iotas(rows, rows)
    leaf = jnp.where(row == column, 1.0, 0.0) - multiply(halves(reflectors_of(vectors_t, inverse)), pair)
    high_ref[:rows], low_ref[:rows] = halves(leaf)
    if low:
        high_ref[rows:], low_ref[rows:] = halves(multiply(halves(vectors_ref[1]), halves(leaf)))


def home_low(low, vectors_ref, own_ref, *refs):
    far_refs, (v_high, v_low) = refs[:low], refs[low:]
    sums = [own_ref[level] + far_refs[level][...] for level in range(low)]
    for level, inverse in enumerate(triangle_inverses(sums)):
        store(v_high, v_low, level, reflectors_of(vectors_ref[1 + level], inverse))


def home_start(chunk, window_ref, high_ref, low_ref, out_ref, *inner_refs):
    rows, wide = out_ref.shape
    result = multiply(operator(high_ref, low_ref), halves(window_ref[:, chunk * wide : (chunk + 1) * wide]))
    out_ref[...] = result[:rows]
    for inner_ref in inner_refs:
        inner_ref[...] = result[rows:]


def home_first(low, window_ref, high_ref, low_ref, vectors_ref, own_ref, *refs):
    far_refs, (v_high, v_low, out_ref, inner_ref) = refs[:low], refs[low:]
    home_low(low, vectors_ref, own_ref, *far_refs, v_high, v_low)
    home_start(0, window_ref, high_ref, low_ref, out_ref, inner_ref)


def tree_operators(held, yt_high, yt_low, v_high, v_low):
    levels, groups = yt_high.shape[:2]
    sums = []
    for level in range(levels):
        apart = 2**level
        gramians = []
        for group in range(groups):
            pair = halves(held(group, level))
            yt_high[level, group], yt_low[level, group] = pair
            gramians.append(multiply(pair, pair, NT))
        sums += [gramians[g] + gramians[g ^ apart] for g in range(groups) if g < g ^ apart]
    inverses = iter(triangle_inverses(sums))
    for level in range(levels):
        apart = 2**level
        for group in range(groups):
            if group < group ^ apart:
                inverse = next(inverses)
                for member in (group, group ^ apart):
                    store(v_high, v_low, (level, member), reflectors_of(held(member, level), inverse))


def top_tree(columns, places, position_ref, near_ref, far_ref, yt_high, yt_low, v_high, v_low, held_ref):
    groups = len(places)
    for group, place in enumerate(places):
        assemble(columns, groups, place, position_ref[0], near_ref, far_ref, held_ref.at[group])
    tree_operators(lambda group, level: held_ref[group, level], yt_high, yt_low, v_high, v_low)


def top_leaf(first, held_ref, a_high, a_low, yt_high, yt_low):
    groups = held_ref.shape[0]
    gramians = []
    for group in range(groups):
        pair = halves(held_ref[group, first])
        gramians.append(multiply(pair, pair, NT))
    row, column = iotas(*a_high.shape[1:])
    for group, inverse in enumerate(triangle_inverses(gramians)):
        vectors_t = held_ref[group, first]
        step = multiply(halves(reflectors_of(vectors_t, inverse)), halves(vectors_t))
        store(a_high, a_low, group, jnp.where(row == column, 1.0, 0.0) - step)
    for level in range(held_ref.shape[1] - first - 1):
        for group in range(groups):
            store(yt_high, yt_low, (level, group), held_ref[group, first + 1 + level])


def top_low(low, late_ref, held_ref, v_high, v_low):
    groups = held_ref.shape[0]
    first, partners = held_ref.shape[1] - low, late_ref.shape[1] - low
    for level in range(low):
        gramians = []
        for group in range(groups):
            pair, partner = halves(held_ref[group, first + level]), halves(late_ref[group, partners + level])
            gramians.append(multiply(pair, pair, NT) + multiply(partner, partner, NT))
        for group, inverse in enumerate(triangle_inverses(gramians)):
            store(v_high, v_low, (level, group), reflectors_of(held_ref[group, first + level], inverse))


def home_level(top_ref, own_ref, far_ref, v_high, v_low, yt_ref, out_ref, inner_ref):
    inner = own_ref[...] + far_ref[...]
    out = top_ref[...] - multiply(operator(v_high, v_low), halves(inner))
    out_ref[...] = out
    inner_ref[...] = multiply(halves(yt_ref[...]), halves(out))


def home_last(groups, position_ref, top_ref, own_ref, far_ref, v_high, v_low, *out_refs):
    width = top_ref.shape[1] // groups
    pair = operator(v_high, v_low)
    for group, out_ref in enumerate(out_refs):
        at = pl.ds(pl.multiple_of((position_ref[0] ^ group) * width, width), width)
        inner = own_ref[:, at] + far_ref[:, at]
        out_ref[...] = top_ref[:, at] - multiply(pair, halves(inner))


def top_levels(tops, levels, yt_high, yt_low, v_high, v_low):
    groups = len(tops)
    for level in range(levels):
        apart = 2**level
        inners = [multiply(operator(yt_high, yt_low, level, g), halves(tops[g])) for g in range(groups)]
        sums = [halves(inners[g] + inners[g ^ apart]) for g in range(groups) if g < g ^ apart]
        order = [g for g in range(groups) if g < g ^ apart]
        tops = [
            tops[g] - multiply(operator(v_high, v_low, level, g), sums[order.index(min(g, g ^ apart))])
            for g in range(groups)
        ]
    return tops


def middle(groups, levels, low, *refs):
    pieces, refs = refs[:groups], refs[groups:]
    yt_high, yt_low, v_high, v_low, a_high, a_low, e_high, e_low = refs[:8]
    out_ref = refs[8]
    tops = top_levels([ref[...] for ref in pieces], levels, yt_high, yt_low, v_high, v_low)
    for g in range(groups):
        top = multiply(operator(a_high, a_low, g), halves(tops[g]))
        out_ref[g] = top
        if low:
            refs[9][g] = multiply(operator(e_high, e_low, 0, g), halves(top))


def low_step(groups, level, top_ref, own_ref, far_ref, v_high, v_low, yt_high, yt_low, out_ref, inner_ref):
    for g in range(groups):
        inner = own_ref[g] + far_ref[g]
        top = top_ref[g] - multiply(operator(v_high, v_low, level, g), halves(inner))
        out_ref[g] = top
        inner_ref[g] = multiply(operator(yt_high, yt_low, level + 1, g), halves(top))


def finish(groups, levels, low, *refs):
    top_ref, refs = refs[0], refs[1:]
    tops = [top_ref[g] for g in range(groups)]
    if low:
        own_ref, far_ref, b_high, b_low = refs[:4]
        refs = refs[4:]
        tops = [
            tops[g] - multiply(operator(b_high, b_low, low - 1, g), halves(own_ref[g] + far_ref[g]))
            for g in range(groups)
        ]
    tops = top_levels(tops, levels, *refs[:4])
    for g, out_ref in enumerate(refs[4:]):
        out_ref[...] = tops[g]


def place(groups, first, count, position_ref, *refs):
    *_, out_ref, sems = refs
    piece_refs = refs[:count]
    width = piece_refs[0].shape[1]
    copies = []
    for at, piece_ref in enumerate(piece_refs):
        where = (first + at // groups * groups + (position_ref[0] ^ (at % groups))) * width
        into = out_ref.at[:, pl.ds(pl.multiple_of(where, width), width)]
        copies.append(pltpu.make_async_copy(piece_ref, into, sems.at[at]))
        copies[-1].start()
    for copy in copies:
        copy.wait()


class Order:
    def __init__(self):
        self.last = None

    def __call__(self, kernel, outs, operands, scalars=0, scratch=(), products=0, copies=0, alias=0):
        in_memory = pl.BlockSpec(memory_space=pltpu.VMEM)
        specs = [pl.BlockSpec(memory_space=pltpu.SMEM)] * scalars + [in_memory] * (len(operands) - scalars)
        shapes = [jax.ShapeDtypeStruct(*out) for out in outs]
        moved = sum(x.size * x.dtype.itemsize for x in [*operands, *shapes])
        held = moved + sum(4 * math.prod(shape) for shape in scratch)
        scratch = [pltpu.VMEM(shape, F32) for shape in scratch]
        out_specs = [in_memory] * len(shapes)
        if copies:
            scratch.append(pltpu.SemaphoreType.DMA((copies,)))
            out_specs = [pl.BlockSpec(memory_space=pl.ANY)] * len(shapes)
        body = kernel
        if alias:
            specs[-1] = pl.BlockSpec(memory_space=pl.ANY)
        if self.last is not None and not alias:
            operands, specs = [self.last, *operands], [pl.BlockSpec(memory_space=pl.ANY), *specs]
            body = lambda token, *refs: kernel(*refs)
        results = pl.pallas_call(
            body,
            out_shape=shapes,
            in_specs=specs,
            out_specs=out_specs,
            scratch_shapes=scratch,
            input_output_aliases={len(operands) - 1: 0} if alias else {},
            name=kernel.func.__name__ if isinstance(kernel, functools.partial) else kernel.__name__,
            compiler_params=pltpu.CompilerParams(vmem_limit_bytes=held + SPARE_BYTES),
            cost_estimate=pl.CostEstimate(
                flops=int(COST * products * 6 * 256**3), bytes_accessed=int(COST * moved), transcendentals=0
            ),
        )(*operands)
        self.last = results[0]
        return results


def swapped(value, axis, mask):
    pairs = [(source, source ^ mask) for source in range(lax.axis_size(axis))]
    return lax.ppermute(value, axis, pairs)


class Gather:
    def __init__(self, value, steps):
        self.value, self.steps = value, list(steps)
        self.send()

    def send(self):
        self.far = swapped(self.value, *self.steps.pop(0))

    @staticmethod
    def step(call, *gathers):
        gathers = [gather for gather in gathers if gather.steps]
        if not gathers:
            return
        shapes = [((2 * g.value.shape[0], *g.value.shape[1:]), F32) for g in gathers]
        joined = call(join, shapes, [x for g in gathers for x in (g.value, g.far)])
        for gather, value in zip(gathers, joined):
            gather.value = value
            gather.send()


def per_device(window, leaf_y, tree_y):
    rows, across = window.shape
    width = tree_y.shape[2]
    groups, low = lax.axis_size("top"), lax.axis_size("low").bit_length() - 1
    top = groups.bit_length() - 1
    column_at = jnp.reshape(lax.axis_index("col"), (1,)).astype(jnp.int32)
    group_at = jnp.reshape(lax.axis_index("top"), (1,)).astype(jnp.int32)
    col_masks = [2**bit for bit in reversed(range(lax.axis_size("col").bit_length() - 1))]
    columns, places = [0], [0]
    for mask in col_masks:
        columns = columns + [offset ^ mask for offset in columns]
    for bit in reversed(range(top)):
        places = places + [offset ^ 2**bit for offset in places]
    places = [places.index(offset) for offset in range(groups)]
    col_steps = [("col", mask) for mask in col_masks]
    all_steps = [("top", 2**bit) for bit in reversed(range(top))] + col_steps
    call = Order()

    leaf_t, tree_t = jnp.swapaxes(leaf_y, 1, 2), jnp.swapaxes(tree_y, 2, 3)
    shard = leaf_t.shape[1]
    home, early, late = call(
        functools.partial(pack, low),
        [((1, count, shard, rows), F32) for count in (1 + low, top + 1 + low, top)],
        [leaf_t, tree_t],
    )
    home, early = Gather(home, col_steps), Gather(early, all_steps)
    partners = [swapped(early.value[0, top + 1 + level], "low", 2**level) for level in range(low)]
    while home.steps:
        Gather.step(call, home)
    vectors, sends = call(
        functools.partial(home_gramians, columns, low),
        [((1 + low, width, rows), F32), ((max(low, 1), width, width), F32)],
        [column_at, home.value, home.far],
        scalars=1,
        products=low,
    )
    leaf = call(
        functools.partial(home_leaf, low), [((rows + (width if low else 0), rows), BF16)] * 2, [vectors], products=8
    )
    chunks = max(1, min(CHUNKS, across // groups // 128))
    wide = across // chunks
    narrow = wide // groups
    piece, stack = ((rows, narrow), F32), ((groups, rows, narrow), F32)
    whole, inner = ((rows, wide), F32), ((width, wide), F32)
    unit = wide / width
    heres, owns, far_inners = [], [], []

    def start(chunk):
        if low and chunk == 0:
            fars = [swapped(sends[level], "low", 2**level) for level in range(low)]
            *low_reflectors, here, own = call(
                functools.partial(home_first, low),
                [((low, rows, width), BF16)] * 2 + [whole, inner],
                [window, *leaf, vectors, sends, *fars],
                products=8 + 2 * unit,
            )
            own = [own]
        else:
            low_reflectors = []
            here, *own = call(
                functools.partial(home_start, chunk), [whole, inner][: 1 + (low > 0)], [window, *leaf], products=2 * unit
            )
        heres.append(here)
        owns.extend(own)
        far_inners.extend(swapped(inner, "low", 1) for inner in own)
        return low_reflectors

    v_high, v_low = start(0) or (None, None)
    if low:
        (late,) = call(extend, [((1, top + low, shard, rows), F32)], [late, *partners])
    Gather.step(call, early)
    late = Gather(late, all_steps)
    Gather.step(call, early, late)

    def give(chunk):
        here = heres[chunk]
        if low:
            own, far = owns[chunk], far_inners[chunk]
            for level in range(low - 1):
                here, own = call(
                    home_level, [whole, inner], [here, own, far, v_high[level], v_low[level], vectors[2 + level]]
                )
                far = swapped(own, "low", 2 ** (level + 1))
            pieces = call(
                functools.partial(home_last, groups),
                [piece] * groups,
                [group_at, here, own, far, v_high[low - 1], v_low[low - 1]],
                scalars=1,
                products=unit,
            )
        else:
            pieces = [
                lax.dynamic_slice_in_dim(here, (group_at[0] ^ g) * narrow, narrow, 1) for g in range(groups)
            ]
        return [pieces[0]] + [swapped(pieces[g], "top", g) for g in range(1, groups)]

    def through(pieces):
        outs = [stack, ((groups, width, narrow), F32)][: 1 + (low > 0)]
        results = call(functools.partial(middle, groups, top, low), outs, [*pieces, *first_ops, *leaf_ops], products=6 * unit)
        return [*results, *([swapped(results[1], "low", 1)] if low else [])]

    def back(state):
        if low:
            here, own, far = state
            for level in range(low - 1):
                here, own = call(
                    functools.partial(low_step, groups, level),
                    [stack, ((groups, width, narrow), F32)],
                    [here, own, far, *low_ops, *leaf_ops[2:]],
                )
                far = swapped(own, "low", 2 ** (level + 1))
            state = [here, own, far, *low_ops]
        pieces = call(functools.partial(finish, groups, top, low), [piece] * groups, [*state, *second_ops], products=5 * unit)
        return [pieces[0]] + [swapped(pieces[g], "top", g) for g in range(1, groups)]

    kept = [((top, groups, width, rows), BF16)] * 2 + [((top, groups, rows, width), BF16)] * 2
    given, states = [], []
    for chunk in range(chunks):
        if chunk + 1 < chunks:
            start(chunk + 1)
        given.append(give(chunk))
        if chunk == 0:
            while early.steps:
                Gather.step(call, early, late)
            *first_ops, held = call(
                functools.partial(top_tree, columns, places),
                [*kept, ((groups, top + 1 + low, width, rows), F32)],
                [column_at, early.value, early.far],
                scalars=1,
                products=32,
            )
            leaf_ops = call(
                functools.partial(top_leaf, top),
                [((groups, rows, rows), BF16)] * 2 + [((max(low, 1), groups, width, rows), BF16)] * 2,
                [held],
                products=32,
            )
        else:
            states.append(through(given[chunk - 1]))
    while late.steps:
        Gather.step(call, late)
    *second_ops, late_held = call(
        functools.partial(top_tree, columns, places),
        [*kept, ((groups, top + low, width, rows), F32)],
        [column_at, late.value, late.far],
        scalars=1,
        products=32,
    )
    if low:
        low_ops = call(
            functools.partial(top_low, low), [((low, groups, rows, width), BF16)] * 2, [late_held, held], products=32 * low
        )
    states.append(through(given[-1]))
    results = []
    for state in states:
        results += back(state)
    done, updated = groups * (chunks - 1), None
    for first, pieces in ((0, results[:done]), (done, results[done:])):
        if pieces:
            kept_out = [] if updated is None else [updated]
            (updated,) = call(
                functools.partial(place, groups, first, len(pieces)),
                [((rows, across), F32)],
                [group_at, *pieces, *kept_out],
                scalars=1,
                copies=len(pieces),
                alias=len(kept_out),
            )
    return updated


def solution(mesh):
    count = mesh.shape["row"]
    groups = min(4, count)
    split = jax.sharding.Mesh(mesh.devices.reshape(groups, count // groups, -1), ("top", "low", "col"))
    row = ("top", "low")
    return jax.shard_map(
        per_device,
        mesh=split,
        in_specs=(P(row, "col"), P(None, row, "col"), P(None, None, row, "col")),
        out_specs=P(row, "col"),
        check_vma=False,
    )
```
